32 devices in a mesh: rep: 8 (over y, x, core), shard: 4 (over z).
Axes of the slice: x: 2, y: 2, z: 4, core: 2. Of those that a mesh axis runs over, the one named last changes fastest.
Arguments:
- tokens: bfloat16 [8192, 768], P(('rep', 'shard')), may hold values from -6 to 6
- cotangent: bfloat16 [8192, 768], P(('rep', 'shard')), may hold values from -6 to 6
- doc_ids: int32 [32, 256], P(('rep', 'shard')), may hold values from 0 to 3, never falling along the last dimension, each value on 1 to 192 neighbouring positions
- buckets: int32 [383], replicated, may hold values from 0 to 31
- routes: int32 [8192, 2], P(('rep', 'shard')), may hold values from 0 to 3, all different within a row; in each aligned block of 256 rows (0 to 255, 256 to 511, ...) at most 256 rows name the same one
- gain_attn: float32 [768], replicated, may hold values from 0.5 to 1.5
- gain_moe: float32 [768], replicated, may hold values from 0.5 to 1.5
- w_query: bfloat16 [768, 768], P('shard'), may hold values from -0.21875 to 0.21875
- w_key: bfloat16 [768, 768], P('shard'), may hold values from -0.21875 to 0.21875
- w_value: bfloat16 [768, 768], P('shard'), may hold values from -0.21875 to 0.21875
- w_proj: bfloat16 [768, 768], P('shard'), may hold values from -0.625 to 0.625
- rel_table: float32 [32, 12], replicated, may hold values from -3 to 3
- w_router: bfloat16 [768, 4], replicated, may hold values from -0.21875 to 0.21875
- w_in: bfloat16 [4, 768, 3072], P('shard'), may hold values from -0.21875 to 0.21875
- w_down: bfloat16 [4, 3072, 768], P('shard'), may hold values from -0.21875 to 0.21875
Outputs:
- mixed: bfloat16 [8192, 768], P(('rep', 'shard'))
- grad_tokens: float32 [8192, 768], P(('rep', 'shard'))
- grad_gain_attn: float32 [768], replicated
- grad_gain_moe: float32 [768], replicated
- grad_query: float32 [768, 768], P('shard')
- grad_key: float32 [768, 768], P('shard')
- grad_value: float32 [768, 768], P('shard')
- grad_proj: float32 [768, 768], P('shard')
- grad_table: float32 [32, 12], replicated
- grad_router: float32 [768, 4], replicated
- grad_in: float32 [4, 768, 3072], P('shard')
- grad_down: float32 [4, 3072, 768], P('shard')
The draws below stay inside these ranges and needn't reach their ends.
Inputs may be any that keep to these rules, and one draw needn't show every extreme that they name: `routes`: each token names two different experts; among the 256 rows of one device no expert is named more than 256 times, and on some devices some expert is named exactly that often.
All inputs are finite; a program needn't handle non-finite values.
Results may differ from the reference program's by a relative error of at most 0.02.
Values may be sent and summed in bfloat16 or wider, within the bound.
A program may use at most 448 MiB of HBM per device.

```python
import math
import jax
import jax.numpy as jnp
import numpy as np
from jax import lax

D = 768
FF = 3072
HEADS = 12
HEAD_DIM = 64
BUCKETS = 32
TOK_DEV = 256
SEQS_DEV = 4
EXPERTS = 4
CAPACITY = 256
MAXLEN = 192
DEVICE_ROWS = 32
TOKENS = 8192


def with_ends(drawn, stream_key, smallest, top_value):
    dims = drawn.shape
    spot = [jax.random.randint(jax.random.fold_in(stream_key, axis), (), 0, dims[axis]) for axis in range(len(dims))]
    drawn = drawn.at[tuple(spot)].set(smallest)
    longest = dims.index(max(dims))
    spot[longest] = (spot[longest] + 1) % dims[longest]
    return drawn.at[tuple(spot)].set(top_value)


def steps_of(own_key, shape, split, smallest, high):
    factor_of = 1.0
    for dim, shards_of in split:
        draws = jax.random.uniform(jax.random.fold_in(jax.random.fold_in(own_key, 6), dim), (shards_of,), jnp.float32, smallest / len(split), high / len(split))
        factor_of = factor_of * jnp.repeat(jnp.exp(draws), shape[dim] // shards_of).reshape((-1,) + (1,) * (len(shape) - 1 - dim))
    return factor_of


def split_up(count, total, reach, lean):
    weights = [(1 << 20) // math.isqrt(grade ** lean) + 1 for grade in range(2, count + 1)]
    surplus, given = total - reach - (count - 1), [1] * (count - 1)
    while surplus > 0:
        free = [i for i in range(count - 1) if given[i] < reach]
        mass, left = sum([weights[i] for i in free]), surplus
        for i in free:
            extra = min(reach - given[i], max(1, left * weights[i] // mass), surplus)
            given[i] = given[i] + extra
            surplus = surplus - extra
    return np.array([reach] + given)


def uneven(own_key, number_of, total, limit, skew):
    if number_of == 2:
        one = jax.random.randint(own_key, (), max(1, total - limit), min(limit, total - 1) + 1)
        return jnp.stack([one, total - one])
    sizes = jnp.asarray(split_up(number_of, total, limit, skew), jnp.int32)
    pairs = (number_of - 1) // 2
    giver, taker = sizes[1:1 + 2 * pairs:2], sizes[2:2 + 2 * pairs:2]
    room = jnp.minimum(giver - 1, limit - taker)
    moved = jax.random.randint(jax.random.fold_in(own_key, 1), (pairs,), 0, 1 << 20) % (room + 1)
    sizes = sizes.at[1:1 + 2 * pairs:2].set(giver - moved).at[2:2 + 2 * pairs:2].set(taker + moved)
    return sizes[jax.random.permutation(jax.random.fold_in(own_key, 2), number_of)]


def routed_block(own_key, own, number, rows, count, top, most, lean):
    sequence = jax.random.permutation(own_key, count)
    crowded, ordinary = shares(count, rows * top, most, lean, True), shares(count, rows * top, most, lean, False)
    places = jnp.arange(count)

    def named(lengths, offset_by):
        used = int((lengths > 0).sum())
        fixed = max(1, used // 4)
        passed = fixed + (places - fixed + offset_by * (used - fixed)) % max(1, count - fixed)
        return jnp.zeros((count,), jnp.int32).at[sequence[jnp.where(places < fixed, places, passed)]].set(jnp.asarray(lengths, jnp.int32))

    lengths = jnp.where(number % 4 == 0, named(crowded, number // 4), named(ordinary, number - number // 4 - 1))
    mixed = jax.random.permutation(jax.random.fold_in(own, 3), count)
    giver, sink = mixed[0:count // 2 * 2:2], mixed[1:count // 2 * 2:2]
    slack = jnp.minimum(lengths[giver] - 1, most - lengths[sink]) // 2
    slack = jnp.where((giver == sequence[0]) | (sink == sequence[0]) | (lengths[sink] == 0), 0, jnp.maximum(slack, 0))
    passed = jax.random.randint(jax.random.fold_in(own, 4), (count // 2,), 0, 1 << 20) % (slack + 1)
    lengths = lengths.at[giver].add(-passed).at[sink].add(passed)
    items = jnp.searchsorted(jnp.cumsum(lengths), jnp.arange(rows * top), side="right").astype(jnp.int32)
    listing = items.reshape(top, rows).T
    listing = listing[jax.random.permutation(jax.random.fold_in(own, 1), rows)]
    offset_by = jax.random.randint(jax.random.fold_in(own, 2), (rows, 1), 0, top)
    return jnp.take_along_axis(listing, (jnp.arange(top)[None, :] + offset_by) % top, axis=1)


def shares(number_of, total, limit, slope, full):
    loads = [(1 << 20) // math.isqrt(standing ** slope) + 1 for standing in range(1, number_of + 1)]
    largest = limit if full else min(limit, max(-(-total // number_of), total * loads[0] // sum(loads)))
    least = 1 if total - largest >= number_of - 1 else 0
    counts, surplus = [largest] + [least] * (number_of - 1), total - largest - least * (number_of - 1)
    while surplus > 0:
        movable = [i for i in range(1, number_of) if counts[i] < largest] or [i for i in range(1, number_of) if counts[i] < limit]
        mass, remaining = sum([loads[i] for i in movable]), surplus
        for i in movable:
            more = min(limit - counts[i], max(1, remaining * loads[i] // mass), surplus)
            counts[i] = counts[i] + more
            surplus = surplus - more
    return np.array(counts)


def gaussian(key, dims, spread, bound, shards=(), held_as=jnp.bfloat16):
    drawn = spread * jax.random.normal(key, dims, jnp.float32)
    if shards:
        drawn = drawn * steps_of(key, dims, shards, -0.22, 0.18)
    return jnp.clip(drawn, -bound, bound).astype(held_as)


def setup_inputs(seed: int = 0) -> dict:
    arg_keys = jax.random.split(jax.random.key(seed), 16)
    tokens = gaussian(arg_keys[0], (TOKENS, D), 1.0, 6.0, ((0, 32),))
    cotangent = gaussian(arg_keys[1], (TOKENS, D), 1.0, 6.0, ((0, 32),))
    doc_ids = jax.vmap(lambda own: jnp.searchsorted(jnp.cumsum(uneven(own, SEQS_DEV, TOK_DEV, MAXLEN, 2)), jnp.arange(TOK_DEV), side="right"))(jax.random.split(arg_keys[2], DEVICE_ROWS)).reshape((DEVICE_ROWS, TOK_DEV)).astype(jnp.int32)
    buckets = with_ends(jax.random.randint(arg_keys[3], (2 * MAXLEN - 1,), 0, BUCKETS), jax.random.fold_in(arg_keys[3], 1), 0, BUCKETS - 1).astype(jnp.int32)
    routes_keys = jax.random.split(jax.random.fold_in(arg_keys[4], 1), TOKENS // TOK_DEV)
    routes_turns = jax.random.permutation(jax.random.fold_in(arg_keys[4], 3), TOKENS // TOK_DEV)
    routes = jax.vmap(lambda own, number: routed_block(jax.random.fold_in(arg_keys[4], 2), own, number, TOK_DEV, EXPERTS, 2, CAPACITY, 1))(routes_keys, routes_turns).reshape((TOKENS, 2))
    gain_attn = jnp.clip(1.0 + 0.1 * jax.random.normal(arg_keys[5], (D,), jnp.float32), 0.5, 1.5)
    gain_moe = jnp.clip(1.0 + 0.1 * jax.random.normal(arg_keys[6], (D,), jnp.float32), 0.5, 1.5)
    w_query = gaussian(arg_keys[7], (D, D), D ** -0.5, 0.21875, ((0, 4),))
    w_key = gaussian(arg_keys[8], (D, D), D ** -0.5, 0.21875, ((0, 4),))
    w_value = gaussian(arg_keys[9], (D, D), D ** -0.5, 0.21875, ((0, 4),))
    w_proj = gaussian(arg_keys[10], (D, D), (D // 8) ** -0.5, 0.625, ((0, 4),))
    rel_table = gaussian(arg_keys[11], (BUCKETS, HEADS), 0.5, 3.0, (), jnp.float32)
    w_router = gaussian(arg_keys[12], (D, EXPERTS), D ** -0.5, 0.21875)
    w_in = gaussian(arg_keys[13], (EXPERTS, D, FF), D ** -0.5, 0.21875, ((0, 4),))
    w_down = gaussian(arg_keys[14], (EXPERTS, FF, D), (FF // 4) ** -0.5, 0.21875, ((0, 4),))
    return {"tokens": tokens, "cotangent": cotangent, "doc_ids": doc_ids, "buckets": buckets, "routes": routes, "gain_attn": gain_attn, "gain_moe": gain_moe, "w_query": w_query, "w_key": w_key, "w_value": w_value, "w_proj": w_proj, "rel_table": rel_table, "w_router": w_router, "w_in": w_in, "w_down": w_down}


EPS = 1e-06

@jax.custom_vjp
def low(v):
    return lax.optimization_barrier(v.astype(jnp.bfloat16)).astype(jnp.float32)

@jax.custom_vjp
def low_back(v):
    return v

def low_keep(v):
    return (low(v), None)

def low_pass(kept, grad):
    return (grad,)

def back_keep(v):
    return (v, None)

def back_low(kept, grad):
    return (low(grad),)
low.defvjp(low_keep, low_pass)
low_back.defvjp(back_keep, back_low)

def exact_dot(left, right):
    return jnp.dot(left, right, precision=lax.Precision.HIGHEST)

def rms_norm(features, gain_vec):
    return features * lax.rsqrt(lax.optimization_barrier(jnp.mean(features * features, axis=-1, keepdims=True)) + EPS) * gain_vec

def position_bias(table_arg, buckets, rows_here):
    span = (buckets.shape[0] + 1) // 2
    steps_idx = jnp.arange(rows_here, dtype=jnp.int32)
    offset = jnp.clip(steps_idx[:, None] - steps_idx[None, :] + span - 1, 0, 2 * span - 2).astype(jnp.int32)
    per_gap = jnp.take(table_arg, buckets, axis=0)
    return jnp.transpose(jnp.take(per_gap, offset, axis=0), (2, 0, 1))

def slot_layout(route_row, experts, capacity):
    flat_routes = route_row.reshape(-1).astype(jnp.int32)
    onehot = (flat_routes[:, None] == jnp.arange(experts, dtype=jnp.int32)[None, :]).astype(jnp.int32)
    before = jnp.cumsum(onehot, axis=0) - onehot
    slot_place = lax.optimization_barrier(jnp.sum(before * onehot, axis=1)).astype(jnp.int32)
    slot_index = (flat_routes * capacity + slot_place).astype(jnp.int32)
    source = (jnp.arange(flat_routes.shape[0], dtype=jnp.int32) // 2).astype(jnp.int32)
    slot_source = jnp.zeros((experts * capacity,), jnp.int32).at[slot_index].set(source)
    filled = jnp.zeros((experts * capacity,), jnp.float32).at[slot_index].set(1.0)
    return (slot_index.reshape(-1, 2), slot_source, filled)

def gate_values(logit_arg, route_row):
    expert_probs = jax.nn.softmax(logit_arg, axis=-1)
    picked = jnp.take_along_axis(expert_probs, route_row, axis=1)
    return picked / lax.optimization_barrier(jnp.sum(picked, axis=1, keepdims=True))

def forward_block(block_in, doc_row, route_row, buckets, gain_attn, gain_moe, w_query, w_key, w_value, w_proj, rel_table, w_router, w_in, w_down):
    rows_here = block_in.shape[0]
    highest = lax.Precision.HIGHEST
    h_first = low(rms_norm(block_in, gain_attn))
    query_low = low(low_back(exact_dot(h_first, w_query))).reshape(rows_here, HEADS, HEAD_DIM)
    keys_low = low(low_back(exact_dot(h_first, w_key))).reshape(rows_here, HEADS, HEAD_DIM)
    values_low = low(low_back(exact_dot(h_first, w_value))).reshape(rows_here, HEADS, HEAD_DIM)
    scores = jnp.einsum('ihd,jhd->hij', query_low, keys_low, precision=highest) * HEAD_DIM ** (-0.5)
    scores = low_back(scores + position_bias(rel_table, buckets, rows_here))
    same_doc = doc_row[:, None] == doc_row[None, :]
    scores = jnp.where(same_doc[None], scores, -1e+30)
    attn_probs = low(jax.nn.softmax(scores, axis=-1))
    mixed_heads = jnp.einsum('hij,jhd->ihd', attn_probs, values_low, precision=highest).reshape(rows_here, D)
    mixed_heads = low(low_back(mixed_heads))
    y_first = block_in + low_back(exact_dot(mixed_heads, w_proj))
    h_second = low(rms_norm(y_first, gain_moe))
    gates = gate_values(exact_dot(h_second, w_router), route_row)
    slot_index, slot_source, filled = slot_layout(route_row, EXPERTS, CAPACITY)
    slot_rows = (low_back(h_second[slot_source]) * filled[:, None]).reshape(EXPERTS, CAPACITY, D)
    hidden = low_back(jnp.einsum('ecd,edf->ecf', slot_rows, w_in, precision=highest))
    act_low = low(jax.nn.gelu(hidden))
    expert_out = low(low_back(jnp.einsum('ecf,efd->ecd', act_low, w_down, precision=highest)))
    expert_out = expert_out.reshape(EXPERTS * CAPACITY, D)
    picked_rows = expert_out[slot_index.reshape(-1)].reshape(rows_here, 2, D)
    return y_first + lax.optimization_barrier(jnp.sum(gates[:, :, None] * picked_rows, axis=1))

def reference(tokens, cotangent, doc_ids, buckets, routes, gain_attn, gain_moe, w_query, w_key, w_value, w_proj, rel_table, w_router, w_in, w_down):
    weights = tuple((weight_arg.astype(jnp.float32) for weight_arg in (gain_attn, gain_moe, w_query, w_key, w_value, w_proj, rel_table, w_router, w_in, w_down)))
    inputs = tokens.astype(jnp.float32).reshape(DEVICE_ROWS, TOK_DEV, D)
    grads_in = cotangent.astype(jnp.float32).reshape(DEVICE_ROWS, TOK_DEV, D)
    route_rows = routes.reshape(DEVICE_ROWS, TOK_DEV, 2)

    def step_block(grad_total, block_item):
        block_in, block_grad, doc_row, route_row = block_item

        def forward_here(block_arg, *weight_args):
            return forward_block(block_arg, doc_row, route_row, buckets, *weight_args)
        block_out, pull_back = jax.vjp(forward_here, block_in, *weights)
        pulled = pull_back(block_grad)
        grad_total = tuple((total_part + pulled_part for total_part, pulled_part in zip(grad_total, pulled[1:])))
        return (grad_total, (block_out.astype(jnp.bfloat16), pulled[0]))
    zeros_init = tuple((jnp.zeros_like(weight_arg) for weight_arg in weights))
    grad_total, (outputs, input_grads) = lax.scan(step_block, zeros_init, (inputs, grads_in, doc_ids, route_rows))
    mixed = outputs.reshape(TOKENS, D)
    grad_tokens = input_grads.reshape(TOKENS, D)
    return (mixed, grad_tokens, grad_total[0], grad_total[1], grad_total[2], grad_total[3], grad_total[4], grad_total[5], grad_total[6], grad_total[7], grad_total[8], grad_total[9])
```

```python
import functools

import jax
import jax.numpy as jnp
from jax import lax
from jax.experimental import pallas as pl
from jax.experimental.pallas import tpu as pltpu
from jax.sharding import PartitionSpec as P

HEADS = 12
HEAD_DIM = 64
EPS = 1e-06
LOW = jnp.bfloat16


def product(left, right):
    return jnp.dot(left, right, preferred_element_type=jnp.float32)


def inner_left(left, right):
    return lax.dot_general(
        left, right, (((0,), (0,)), ((), ())), preferred_element_type=jnp.float32
    )


def inner_right(left, right):
    return lax.dot_general(
        left, right, (((1,), (1,)), ((), ())), preferred_element_type=jnp.float32
    )


def inverse_rms(features):
    return lax.rsqrt(jnp.mean(features * features, axis=-1, keepdims=True) + EPS)


def rms_pull(features, scale, gain_vec, grad):
    unit = features * scale
    scaled = grad * gain_vec
    grad_features = scale * (scaled - unit * jnp.mean(scaled * unit, axis=-1, keepdims=True))
    return grad_features, jnp.sum(grad * unit, axis=0)


def gap_onehot(buckets, count, width):
    span = (buckets.shape[0] + 1) // 2
    back = jnp.flip(buckets)
    lanes = jnp.concatenate(
        [back[span - 1 :], jnp.full((width - 2 * span + 1,), -1, jnp.int32), back[: span - 1]]
    )
    return (lanes[:, None] == jnp.arange(count, dtype=jnp.int32)[None, :]).astype(jnp.float32)


def sum_onehot(buckets, count, width):
    ahead = width // 2 - (buckets.shape[0] + 1) // 2
    lanes = jnp.pad(
        buckets, (ahead, width - ahead - buckets.shape[0]), constant_values=-1
    )
    return (lanes[:, None] == jnp.arange(count, dtype=jnp.int32)[None, :]).astype(jnp.float32)


def attention_kernel(q_ref, k_ref, v_ref, gap_ref, col_ref, row_ref, p_ref, o_ref):
    rows = q_ref.shape[0]
    same = col_ref[...] == row_ref[...]
    for s in range(2):
        cols = pl.ds(s * HEAD_DIM, HEAD_DIM)
        skew = pltpu.roll(
            jnp.broadcast_to(gap_ref[s], (rows, gap_ref.shape[2])), 0, 1, stride=1, stride_axis=0
        )[:, :rows]
        scores = inner_right(q_ref[:, cols], k_ref[:, cols]) * HEAD_DIM ** (-0.5)
        scores = jnp.where(same, scores + skew, -1e30)
        grown = jnp.exp(scores - jnp.max(scores, axis=-1, keepdims=True))
        probs = grown / jnp.sum(grown, axis=-1, keepdims=True)
        p_ref[s] = probs
        o_ref[:, cols] = product(probs.astype(LOW), v_ref[:, cols]).astype(LOW)


def attention(qkv, gaps, doc_row):
    rows = qkv.shape[0]
    width = gaps.shape[2]
    pairs = HEADS // 2
    two = 2 * HEAD_DIM

    def part(n):
        return pl.BlockSpec((rows, two), lambda h: (0, n * pairs + h))

    return pl.pallas_call(
        attention_kernel,
        grid=(pairs,),
        in_specs=[
            part(0),
            part(1),
            part(2),
            pl.BlockSpec((2, 1, width), lambda h: (h, 0, 0)),
            pl.BlockSpec((rows, 1), lambda h: (0, 0)),
            pl.BlockSpec((1, rows), lambda h: (0, 0)),
        ],
        out_specs=[pl.BlockSpec((2, rows, rows), lambda h: (h, 0, 0)), part(0)],
        out_shape=[
            jax.ShapeDtypeStruct((HEADS, rows, rows), jnp.float32),
            jax.ShapeDtypeStruct((rows, HEADS * HEAD_DIM), LOW),
        ],
        compiler_params=pltpu.CompilerParams(vmem_limit_bytes=32 * 1024 * 1024),
        cost_estimate=pl.CostEstimate(
            flops=4 * HEADS * rows * rows * HEAD_DIM,
            bytes_accessed=4 * HEADS * rows * rows,
            transcendentals=HEADS * rows * rows,
        ),
    )(qkv, qkv, qkv, gaps, doc_row.reshape(-1, 1), doc_row.reshape(1, -1))


def attention_back_kernel(q_ref, k_ref, v_ref, p_ref, g_ref, gq_ref, gk_ref, gv_ref, gap_ref):
    rows = q_ref.shape[0]
    width = gap_ref.shape[2]
    scale = HEAD_DIM ** (-0.5)
    down = lax.broadcasted_iota(jnp.int32, (rows, rows), 0)
    across = lax.broadcasted_iota(jnp.int32, (rows, rows), 1)
    mirror = (down + across == rows - 1).astype(LOW)
    for s in range(2):
        cols = pl.ds(s * HEAD_DIM, HEAD_DIM)
        probs = p_ref[s]
        out_grad = g_ref[:, cols]
        grad_p = inner_right(out_grad, v_ref[:, cols])
        gv_ref[:, cols] = inner_left(probs.astype(LOW), out_grad).astype(LOW)
        grad_s = probs * (grad_p - jnp.sum(grad_p * probs, axis=-1, keepdims=True))
        grad_low = grad_s.astype(LOW)
        gq_ref[:, cols] = (product(grad_low, k_ref[:, cols]) * scale).astype(LOW)
        gk_ref[:, cols] = (inner_left(grad_low, q_ref[:, cols]) * scale).astype(LOW)
        wide = jnp.concatenate(
            [product(grad_low, mirror), jnp.zeros((rows, width - rows), jnp.float32)], axis=1
        )
        straight = pltpu.roll(wide, 0, 1, stride=1, stride_axis=0)
        gap_ref[s] = jnp.sum(straight, axis=0, keepdims=True)


def attention_back(qkv, probs, grad_heads, width):
    rows = qkv.shape[0]
    pairs = HEADS // 2
    two = 2 * HEAD_DIM

    def part(n):
        return pl.BlockSpec((rows, two), lambda h: (0, n * pairs + h))

    flat = jax.ShapeDtypeStruct((rows, HEADS * HEAD_DIM), LOW)
    return pl.pallas_call(
        attention_back_kernel,
        grid=(pairs,),
        in_specs=[
            part(0),
            part(1),
            part(2),
            pl.BlockSpec((2, rows, rows), lambda h: (h, 0, 0)),
            part(0),
        ],
        out_specs=[
            part(0),
            part(0),
            part(0),
            pl.BlockSpec((2, 1, width), lambda h: (h, 0, 0)),
        ],
        out_shape=[flat, flat, flat, jax.ShapeDtypeStruct((HEADS, 1, width), jnp.float32)],
        compiler_params=pltpu.CompilerParams(vmem_limit_bytes=32 * 1024 * 1024),
        cost_estimate=pl.CostEstimate(
            flops=8 * HEADS * rows * rows * HEAD_DIM,
            bytes_accessed=4 * HEADS * rows * rows,
            transcendentals=0,
        ),
    )(qkv, qkv, qkv, probs, grad_heads)


def gather_projections(stacked, rep, piece):
    part = lax.dynamic_slice_in_dim(stacked, rep * piece, piece, axis=0)
    return lax.all_gather(part, ("shard", "rep"), axis=0, tiled=True)


def reduce_projections(whole):
    return lax.psum_scatter(whole, ("shard", "rep"), scatter_dimension=0, tiled=True)


def on_device(
    tokens,
    cotangent,
    doc_ids,
    buckets,
    routes,
    gain_attn,
    gain_moe,
    w_query,
    w_key,
    w_value,
    w_proj,
    rel_table,
    w_router,
    w_in,
    w_down,
):
    rows_here, model = tokens.shape
    reps = lax.axis_size("rep")
    rep = lax.axis_index("rep")
    mine = lax.axis_index("shard")
    width = 2 * rows_here
    inputs = tokens.astype(jnp.float32)

    stacked = jnp.concatenate([w_query, w_key, w_value, w_proj], axis=1)
    piece = stacked.shape[0] // reps
    full = gather_projections(stacked, rep, piece)
    all_cot = lax.all_gather(cotangent, "shard", axis=0, tiled=True)
    all_routes = lax.all_gather(routes, "shard", axis=0, tiled=True)

    onehot = gap_onehot(buckets, rel_table.shape[0], width)
    gaps = lax.dot_general(
        rel_table, onehot, (((0,), (1,)), ((), ())), precision=lax.Precision.HIGHEST
    ).reshape(HEADS, 1, width)
    scale_first = inverse_rms(inputs)
    h_first = (inputs * scale_first * gain_attn).astype(LOW)
    full_qkv = full[:, : 3 * model]
    full_proj = full[:, 3 * model :]
    qkv = product(h_first, full_qkv).astype(LOW)
    probs, mixed_heads = attention(qkv, gaps, doc_ids[0])
    y_first = inputs + product(mixed_heads, full_proj)
    scale_second = inverse_rms(y_first)
    h_second = (y_first * scale_second * gain_moe).astype(LOW)

    all_h = lax.all_gather(h_second, "shard", axis=0, tiled=True)
    logits = product(all_h, w_router)
    ids = jnp.arange(w_router.shape[1], dtype=jnp.int32)[None, :]
    hot_first = (all_routes[:, 0:1] == ids).astype(jnp.float32)
    hot_second = (all_routes[:, 1:2] == ids).astype(jnp.float32)
    apart = hot_first - hot_second
    gap_logit = jnp.sum(logits * apart, axis=1, keepdims=True)
    gate_first = jax.nn.sigmoid(gap_logit)
    gate_second = jax.nn.sigmoid(-gap_logit)
    is_first = (all_routes[:, 0:1] == mine).astype(jnp.float32)
    is_second = (all_routes[:, 1:2] == mine).astype(jnp.float32)
    gate = is_first * gate_first + is_second * gate_second
    out_grad_all = all_cot.astype(jnp.float32)
    grad_eo = (out_grad_all * gate).astype(LOW)

    w_first, w_second = w_in[0], w_down[0]
    hidden = product(all_h, w_first)
    act_full, gelu_pull = jax.vjp(jax.nn.gelu, hidden)
    act_low = act_full.astype(LOW)
    grad_act = inner_right(grad_eo, w_second)
    grad_hidden = gelu_pull(grad_act)[0].astype(LOW)
    expert_out = product(act_low, w_second).astype(LOW).astype(jnp.float32)
    grad_rows = inner_right(grad_hidden, w_first)
    grad_gate = jnp.sum(out_grad_all * expert_out, axis=1, keepdims=True)
    grad_gap = grad_gate * (is_first - is_second) * gate_first * gate_second
    grad_logits = grad_gap * apart
    grad_router = lax.dot_general(
        all_h.astype(jnp.float32),
        grad_logits,
        (((0,), (0,)), ((), ())),
        precision=lax.Precision.HIGHEST,
    )
    back_h = grad_rows + lax.dot_general(
        grad_logits,
        w_router.astype(jnp.float32),
        (((1,), (1,)), ((), ())),
        precision=lax.Precision.HIGHEST,
    )
    grad_h_second = lax.psum_scatter(
        back_h.astype(LOW), "shard", scatter_dimension=0, tiled=True
    ).astype(jnp.float32)

    grad_down = inner_left(act_low, grad_eo).astype(LOW)
    grad_in = inner_left(all_h, grad_hidden).astype(LOW)
    part_down = lax.psum_scatter(grad_down, "rep", scatter_dimension=0, tiled=True)
    part_in = lax.psum_scatter(grad_in, "rep", scatter_dimension=0, tiled=True)
    routed = lax.psum_scatter(
        (gate * expert_out).astype(LOW), "shard", scatter_dimension=0, tiled=True
    ).astype(jnp.float32)
    mixed = (y_first + routed).astype(LOW)

    out_grad = cotangent.astype(jnp.float32)
    grad_y_part, grad_gain_moe = rms_pull(y_first, scale_second, gain_moe, grad_h_second)
    grad_y_first = out_grad + grad_y_part
    grad_attn = grad_y_first.astype(LOW)
    grad_heads = inner_right(grad_attn, full_proj).astype(LOW)
    grad_q, grad_k, grad_v, grad_gap_sums = attention_back(qkv, probs, grad_heads, width)
    grad_table = lax.dot_general(
        sum_onehot(buckets, rel_table.shape[0], width),
        grad_gap_sums.reshape(HEADS, width),
        (((0,), (1,)), ((), ())),
        precision=lax.Precision.HIGHEST,
    )
    grad_qkv = jnp.concatenate([grad_q, grad_k, grad_v], axis=1)
    grad_h_first = inner_right(grad_qkv, full_qkv)
    whole = jnp.concatenate(
        [inner_left(h_first, grad_qkv).astype(LOW), inner_left(mixed_heads, grad_attn).astype(LOW)],
        axis=1,
    )
    own = reduce_projections(whole)
    grad_x_part, grad_gain_attn = rms_pull(inputs, scale_first, gain_attn, grad_h_first)
    grad_tokens = grad_y_first + grad_x_part

    sum_down = lax.all_gather(part_down, "rep", axis=0, tiled=True).astype(jnp.float32)
    sum_in = lax.all_gather(part_in, "rep", axis=0, tiled=True).astype(jnp.float32)
    own = lax.all_gather(own, "rep", axis=0, tiled=True).astype(jnp.float32)
    small = jnp.concatenate(
        [
            grad_gain_attn,
            grad_gain_moe,
            grad_router.reshape(-1),
            grad_table.reshape(-1),
        ]
    )
    cut = small.shape[0]
    lines = -(-cut // 1024) * 8
    small = jnp.pad(small, (0, lines * 128 - cut)).reshape(lines, 128)
    small = lax.psum(small, ("rep", "shard")).reshape(-1)
    marks = [model, 2 * model, 2 * model + w_router.size]
    sum_gain_attn, sum_gain_moe, sum_router, sum_table = jnp.split(small[:cut], marks)
    return (
        mixed,
        grad_tokens,
        sum_gain_attn,
        sum_gain_moe,
        own[:, :model],
        own[:, model : 2 * model],
        own[:, 2 * model : 3 * model],
        own[:, 3 * model :],
        sum_table.reshape(rel_table.shape),
        sum_router.reshape(w_router.shape),
        sum_in[None],
        sum_down[None],
    )


def solution(mesh):
    in_specs = (
        P(("rep", "shard"), None),
        P(("rep", "shard"), None),
        P(("rep", "shard"), None),
        P(),
        P(("rep", "shard"), None),
        P(),
        P(),
        P("shard", None),
        P("shard", None),
        P("shard", None),
        P("shard", None),
        P(),
        P(),
        P("shard", None, None),
        P("shard", None, None),
    )
    out_specs = (
        P(("rep", "shard"), None),
        P(("rep", "shard"), None),
        P(),
        P(),
        P("shard", None),
        P("shard", None),
        P("shard", None),
        P("shard", None),
        P(),
        P(),
        P("shard", None, None),
        P("shard", None, None),
    )
    return jax.shard_map(
        on_device, mesh=mesh, in_specs=in_specs, out_specs=out_specs, check_vma=False
    )
```

```python
import functools

import jax
import jax.numpy as jnp
from jax import lax
from jax.experimental import pallas as pl
from jax.experimental.pallas import tpu as pltpu
from jax.sharding import PartitionSpec as P

HEADS = 12
HEAD_DIM = 64
EPS = 1e-06
LOW = jnp.bfloat16


def product(left, right):
    return jnp.dot(left, right, preferred_element_type=jnp.float32)


def inner_left(left, right):
    return lax.dot_general(
        left, right, (((0,), (0,)), ((), ())), preferred_element_type=jnp.float32
    )


def inner_right(left, right):
    return lax.dot_general(
        left, right, (((1,), (1,)), ((), ())), preferred_element_type=jnp.float32
    )


def inverse_rms(features):
    return lax.rsqrt(jnp.mean(features * features, axis=-1, keepdims=True) + EPS)


def rms_pull(features, scale, gain_vec, grad):
    unit = features * scale
    scaled = grad * gain_vec
    grad_features = scale * (scaled - unit * jnp.mean(scaled * unit, axis=-1, keepdims=True))
    return grad_features, jnp.sum(grad * unit, axis=0)


def gap_onehot(buckets, count, width):
    span = (buckets.shape[0] + 1) // 2
    back = jnp.flip(buckets)
    lanes = jnp.concatenate(
        [back[span - 1 :], jnp.full((width - 2 * span + 1,), -1, jnp.int32), back[: span - 1]]
    )
    return (lanes[:, None] == jnp.arange(count, dtype=jnp.int32)[None, :]).astype(jnp.float32)


def sum_onehot(buckets, count, width):
    ahead = width // 2 - (buckets.shape[0] + 1) // 2
    lanes = jnp.pad(
        buckets, (ahead, width - ahead - buckets.shape[0]), constant_values=-1
    )
    return (lanes[:, None] == jnp.arange(count, dtype=jnp.int32)[None, :]).astype(jnp.float32)


def attention_kernel(q_ref, k_ref, v_ref, gap_ref, col_ref, row_ref, p_ref, o_ref):
    rows = q_ref.shape[0]
    same = col_ref[...] == row_ref[...]
    for s in range(2):
        cols = pl.ds(s * HEAD_DIM, HEAD_DIM)
        skew = pltpu.roll(
            jnp.broadcast_to(gap_ref[s], (rows, gap_ref.shape[2])), 0, 1, stride=1, stride_axis=0
        )[:, :rows]
        scores = inner_right(q_ref[:, cols], k_ref[:, cols]) * HEAD_DIM ** (-0.5)
        scores = jnp.where(same, scores + skew, -1e30)
        grown = jnp.exp(scores - jnp.max(scores, axis=-1, keepdims=True))
        probs = grown / jnp.sum(grown, axis=-1, keepdims=True)
        p_ref[s] = probs
        o_ref[:, cols] = product(probs.astype(LOW), v_ref[:, cols]).astype(LOW)


def attention(qkv, gaps, doc_row):
    rows = qkv.shape[0]
    width = gaps.shape[2]
    pairs = HEADS // 2
    two = 2 * HEAD_DIM

    def part(n):
        return pl.BlockSpec((rows, two), lambda h: (0, n * pairs + h))

    return pl.pallas_call(
        attention_kernel,
        grid=(pairs,),
        in_specs=[
            part(0),
            part(1),
            part(2),
            pl.BlockSpec((2, 1, width), lambda h: (h, 0, 0)),
            pl.BlockSpec((rows, 1), lambda h: (0, 0)),
            pl.BlockSpec((1, rows), lambda h: (0, 0)),
        ],
        out_specs=[pl.BlockSpec((2, rows, rows), lambda h: (h, 0, 0)), part(0)],
        out_shape=[
            jax.ShapeDtypeStruct((HEADS, rows, rows), jnp.float32),
            jax.ShapeDtypeStruct((rows, HEADS * HEAD_DIM), LOW),
        ],
        compiler_params=pltpu.CompilerParams(vmem_limit_bytes=32 * 1024 * 1024),
        cost_estimate=pl.CostEstimate(
            flops=4 * HEADS * rows * rows * HEAD_DIM,
            bytes_accessed=4 * HEADS * rows * rows,
            transcendentals=HEADS * rows * rows,
        ),
    )(qkv, qkv, qkv, gaps, doc_row.reshape(-1, 1), doc_row.reshape(1, -1))


def attention_back_kernel(q_ref, k_ref, v_ref, p_ref, g_ref, gq_ref, gk_ref, gv_ref, gap_ref):
    rows = q_ref.shape[0]
    width = gap_ref.shape[2]
    scale = HEAD_DIM ** (-0.5)
    down = lax.broadcasted_iota(jnp.int32, (rows, rows), 0)
    across = lax.broadcasted_iota(jnp.int32, (rows, rows), 1)
    mirror = (down + across == rows - 1).astype(LOW)
    for s in range(2):
        cols = pl.ds(s * HEAD_DIM, HEAD_DIM)
        probs = p_ref[s]
        out_grad = g_ref[:, cols]
        grad_p = inner_right(out_grad, v_ref[:, cols])
        gv_ref[:, cols] = inner_left(probs.astype(LOW), out_grad).astype(LOW)
        grad_s = probs * (grad_p - jnp.sum(grad_p * probs, axis=-1, keepdims=True))
        grad_low = grad_s.astype(LOW)
        gq_ref[:, cols] = (product(grad_low, k_ref[:, cols]) * scale).astype(LOW)
        gk_ref[:, cols] = (inner_left(grad_low, q_ref[:, cols]) * scale).astype(LOW)
        wide = jnp.concatenate(
            [product(grad_low, mirror), jnp.zeros((rows, width - rows), jnp.float32)], axis=1
        )
        straight = pltpu.roll(wide, 0, 1, stride=1, stride_axis=0)
        gap_ref[s] = jnp.sum(straight, axis=0, keepdims=True)


def attention_back(qkv, probs, grad_heads, width):
    rows = qkv.shape[0]
    pairs = HEADS // 2
    two = 2 * HEAD_DIM

    def part(n):
        return pl.BlockSpec((rows, two), lambda h: (0, n * pairs + h))

    flat = jax.ShapeDtypeStruct((rows, HEADS * HEAD_DIM), LOW)
    return pl.pallas_call(
        attention_back_kernel,
        grid=(pairs,),
        in_specs=[
            part(0),
            part(1),
            part(2),
            pl.BlockSpec((2, rows, rows), lambda h: (h, 0, 0)),
            part(0),
        ],
        out_specs=[
            part(0),
            part(0),
            part(0),
            pl.BlockSpec((2, 1, width), lambda h: (h, 0, 0)),
        ],
        out_shape=[flat, flat, flat, jax.ShapeDtypeStruct((HEADS, 1, width), jnp.float32)],
        compiler_params=pltpu.CompilerParams(vmem_limit_bytes=32 * 1024 * 1024),
        cost_estimate=pl.CostEstimate(
            flops=8 * HEADS * rows * rows * HEAD_DIM,
            bytes_accessed=4 * HEADS * rows * rows,
            transcendentals=0,
        ),
    )(qkv, qkv, qkv, probs, grad_heads)


def gather_projections(part):
    return lax.all_gather(part, ("shard", "rep"), axis=0, tiled=True)


def turn(block, step):
    count = lax.axis_size("shard")
    return lax.ppermute(block, "shard", [(d, (d + step) % count) for d in range(count)])


def swap(block, axis_name, bit):
    count = lax.axis_size(axis_name)
    return lax.ppermute(block, axis_name, [(d, d ^ bit) for d in range(count)])


def spans(axis_name):
    count = lax.axis_size(axis_name)
    return [1 << b for b in range(count.bit_length() - 1)]


def halve_sum(block, axis):
    rep = lax.axis_index("rep")
    for bit in spans("rep"):
        upper = (rep // bit) % 2
        half = block.shape[axis] // 2
        kept = lax.dynamic_slice_in_dim(block, upper * half, half, axis)
        sent = lax.dynamic_slice_in_dim(block, (1 - upper) * half, half, axis)
        came = swap(sent, "rep", bit)
        block = (kept.astype(jnp.float32) + came.astype(jnp.float32)).astype(LOW)
    return block


def double_up(block):
    rep = lax.axis_index("rep")
    for bit in reversed(spans("rep")):
        upper = (rep // bit) % 2 == 1
        came = swap(block, "rep", bit)
        block = jnp.concatenate(
            [jnp.where(upper, came, block), jnp.where(upper, block, came)], axis=0
        )
    return block


def sum_everywhere(small):
    for axis_name in ("rep", "shard"):
        for bit in spans(axis_name):
            small = small + swap(small, axis_name, bit)
    return small


def reduce_projections(whole):
    count = lax.axis_size("shard")
    mine = lax.axis_index("shard")
    held = halve_sum(whole.reshape(count, -1, whole.shape[1]), 1)
    total = lax.dynamic_index_in_dim(held, mine, 0, keepdims=False).astype(jnp.float32)
    for step in range(1, count):
        block = lax.dynamic_index_in_dim(held, (mine + step) % count, 0, keepdims=False)
        total = total + turn(block, step).astype(jnp.float32)
    return total.astype(LOW)


def on_device(
    tokens,
    cotangent,
    doc_ids,
    buckets,
    routes,
    gain_attn,
    gain_moe,
    w_query,
    w_key,
    w_value,
    w_proj,
    rel_table,
    w_router,
    w_in,
    w_down,
):
    rows_here, model = tokens.shape
    reps = lax.axis_size("rep")
    rep = lax.axis_index("rep")
    mine = lax.axis_index("shard")
    width = 2 * rows_here
    inputs = tokens.astype(jnp.float32)

    shards = lax.axis_size("shard")
    piece = w_query.shape[0] // reps
    parts = [
        lax.dynamic_slice_in_dim(w, rep * piece, piece, axis=0)
        for w in (w_query, w_key, w_value, w_proj)
    ]
    full_qkv = gather_projections(jnp.concatenate(parts[:3], axis=1))
    full_proj = gather_projections(parts[3])
    cot_blocks = [cotangent] + [turn(cotangent, step) for step in range(1, shards)]
    route_blocks = [routes] + [turn(routes, step) for step in range(1, shards)]

    onehot = gap_onehot(buckets, rel_table.shape[0], width)
    gaps = lax.dot_general(
        rel_table, onehot, (((0,), (1,)), ((), ())), precision=lax.Precision.HIGHEST
    ).reshape(HEADS, 1, width)
    scale_first = inverse_rms(inputs)
    h_first = (inputs * scale_first * gain_attn).astype(LOW)
    qkv = product(h_first, full_qkv).astype(LOW)
    probs, mixed_heads = attention(qkv, gaps, doc_ids[0])
    y_first = inputs + product(mixed_heads, full_proj)
    scale_second = inverse_rms(y_first)
    h_second = (y_first * scale_second * gain_moe).astype(LOW)

    h_blocks = [h_second] + [turn(h_second, step) for step in range(1, shards)]
    w_first, w_second = w_in[0], w_down[0]
    ids = jnp.arange(w_router.shape[1], dtype=jnp.int32)[None, :]
    acts, grads_eo, grads_hidden, grads_logits = [], [], [], []
    grad_h_second = jnp.zeros((rows_here, model), jnp.float32)
    routed = jnp.zeros((rows_here, model), jnp.float32)
    for step in range(shards):
        h_here, route = h_blocks[step], route_blocks[step]
        out_grad_here = cot_blocks[step].astype(jnp.float32)
        logits = product(h_here, w_router)
        apart = (route[:, 0:1] == ids).astype(jnp.float32) - (route[:, 1:2] == ids).astype(
            jnp.float32
        )
        gap_logit = jnp.sum(logits * apart, axis=1, keepdims=True)
        gate_first = jax.nn.sigmoid(gap_logit)
        gate_second = jax.nn.sigmoid(-gap_logit)
        is_first = (route[:, 0:1] == mine).astype(jnp.float32)
        is_second = (route[:, 1:2] == mine).astype(jnp.float32)
        gate = is_first * gate_first + is_second * gate_second
        grad_eo = (out_grad_here * gate).astype(LOW)
        act_full, gelu_pull = jax.vjp(jax.nn.gelu, product(h_here, w_first))
        act_low = act_full.astype(LOW)
        grad_hidden = gelu_pull(inner_right(grad_eo, w_second))[0].astype(LOW)
        expert_out = product(act_low, w_second).astype(LOW).astype(jnp.float32)
        grad_gate = jnp.sum(out_grad_here * expert_out, axis=1, keepdims=True)
        grad_logits = grad_gate * (is_first - is_second) * gate_first * gate_second * apart
        back_h = inner_right(grad_hidden, w_first) + lax.dot_general(
            grad_logits,
            w_router.astype(jnp.float32),
            (((1,), (1,)), ((), ())),
            precision=lax.Precision.HIGHEST,
        )
        out_here = gate * expert_out
        if step:
            back_h = turn(back_h.astype(LOW), shards - step).astype(jnp.float32)
            out_here = turn(out_here.astype(LOW), shards - step).astype(jnp.float32)
        grad_h_second = grad_h_second + back_h
        routed = routed + out_here
        acts.append(act_low)
        grads_eo.append(grad_eo)
        grads_hidden.append(grad_hidden)
        grads_logits.append(grad_logits)
    all_h = jnp.concatenate(h_blocks, axis=0)
    grad_down = inner_left(jnp.concatenate(acts, axis=0), jnp.concatenate(grads_eo, axis=0))
    grad_in = inner_left(all_h, jnp.concatenate(grads_hidden, axis=0))
    part_in = lax.psum_scatter(grad_in.astype(LOW), "rep", scatter_dimension=0, tiled=True)
    sum_in = lax.all_gather(part_in, "rep", axis=0, tiled=True).astype(jnp.float32)
    part_down = halve_sum(grad_down.astype(LOW), 0)
    grad_router = lax.dot_general(
        all_h.astype(jnp.float32),
        jnp.concatenate(grads_logits, axis=0),
        (((0,), (0,)), ((), ())),
        precision=lax.Precision.HIGHEST,
    )
    mixed = (y_first + routed).astype(LOW)

    out_grad = cotangent.astype(jnp.float32)
    grad_y_part, grad_gain_moe = rms_pull(y_first, scale_second, gain_moe, grad_h_second)
    grad_y_first = out_grad + grad_y_part
    grad_attn = grad_y_first.astype(LOW)
    grad_heads = inner_right(grad_attn, full_proj).astype(LOW)
    grad_q, grad_k, grad_v, grad_gap_sums = attention_back(qkv, probs, grad_heads, width)
    grad_table = lax.dot_general(
        sum_onehot(buckets, rel_table.shape[0], width),
        grad_gap_sums.reshape(HEADS, width),
        (((0,), (1,)), ((), ())),
        precision=lax.Precision.HIGHEST,
    )
    grad_qkv = jnp.concatenate([grad_q, grad_k, grad_v], axis=1)
    grad_h_first = inner_right(grad_qkv, full_qkv)
    whole = jnp.concatenate(
        [inner_left(h_first, grad_qkv).astype(LOW), inner_left(mixed_heads, grad_attn).astype(LOW)],
        axis=1,
    )
    own = reduce_projections(whole)
    grad_x_part, grad_gain_attn = rms_pull(inputs, scale_first, gain_attn, grad_h_first)
    grad_tokens = grad_y_first + grad_x_part

    sum_down = double_up(part_down).astype(jnp.float32)
    own = double_up(own).astype(jnp.float32)
    small = jnp.concatenate(
        [
            grad_gain_attn,
            grad_gain_moe,
            grad_router.reshape(-1),
            grad_table.reshape(-1),
        ]
    )
    cut = small.shape[0]
    lines = -(-cut // 1024) * 8
    small = jnp.pad(small, (0, lines * 128 - cut)).reshape(lines, 128)
    small = sum_everywhere(small).reshape(-1)
    marks = [model, 2 * model, 2 * model + w_router.size]
    sum_gain_attn, sum_gain_moe, sum_router, sum_table = jnp.split(small[:cut], marks)
    return (
        mixed,
        grad_tokens,
        sum_gain_attn,
        sum_gain_moe,
        own[:, :model],
        own[:, model : 2 * model],
        own[:, 2 * model : 3 * model],
        own[:, 3 * model :],
        sum_table.reshape(rel_table.shape),
        sum_router.reshape(w_router.shape),
        sum_in[None],
        sum_down[None],
    )


def solution(mesh):
    in_specs = (
        P(("rep", "shard"), None),
        P(("rep", "shard"), None),
        P(("rep", "shard"), None),
        P(),
        P(("rep", "shard"), None),
        P(),
        P(),
        P("shard", None),
        P("shard", None),
        P("shard", None),
        P("shard", None),
        P(),
        P(),
        P("shard", None, None),
        P("shard", None, None),
    )
    out_specs = (
        P(("rep", "shard"), None),
        P(("rep", "shard"), None),
        P(),
        P(),
        P("shard", None),
        P("shard", None),
        P("shard", None),
        P("shard", None),
        P(),
        P(),
        P("shard", None, None),
        P("shard", None, None),
    )
    return jax.shard_map(
        on_device, mesh=mesh, in_specs=in_specs, out_specs=out_specs, check_vma=False
    )
```
